32 devices in a mesh: real: 2 (over x), space: 8 (over z, y), sub: 2 (over core).
Axes of the slice: x: 2, y: 2, z: 4, core: 2. Of those that a mesh axis runs over, the one named last changes fastest.
Arguments:
- force: float32 [4096, 384], P(('real', 'space')), parts along dimension 0, may hold values from -12 to 12
- drag: float32 [4096, 384], P(('real', 'space')), parts along dimension 0, may hold values from 0.5 to 2
- mode_matrix: float32 [6, 6], replicated, may hold values from -0.4 to 3, as said below
- tile_rows: int32 [8192], P(('real', 'space', 'sub')), parts along dimension 0, may hold values from 0 to 255
- tile_cols: int32 [8192], P(('real', 'space', 'sub')), parts along dimension 0, may hold values from 0 to 287
- gaps: bfloat16 [8192, 4096], P(('real', 'space', 'sub')), parts along dimension 0, may hold values from 0.0099487305 to 1
- send_blocks: int32 [16, 8, 4], P(('real', 'space')), parts along dimension 0, may hold values from 0 to 255
Outputs:
- velocity: float32 [4096, 384], P(('real', 'space')), parts along dimension 0
- residual: float32 [4096, 384], P(('real', 'space')), parts along dimension 0
The draws below stay inside these ranges and needn't reach their ends.
There are 2 independent parts, one for each index of `real`. The reference program is written for one: setup_inputs(seed, part) draws one part's arguments, and reference() takes and returns one part's arrays. A program takes and returns all parts, laid end to end along the dimension named above; an argument that names none is the same for every part. Nothing has to cross between parts.
Inputs may be any that keep to these rules, and one draw needn't show every extreme that they name: `mode_matrix`: symmetric; every diagonal entry exceeds the sum of magnitudes of the other entries of its row.
All inputs are finite; a program needn't handle non-finite values.
Results may differ from the reference program's by a relative error of at most 0.0003.
Values sent between devices are 32-bit elements; how exact they have to be, the bound alone decides.
A program may use at most 64 MiB of HBM per device.

```python
import math
import jax
import jax.numpy as jnp
from jax import lax

BLOCK = 64
BLK_DEV = 256
TILE_DEV = 256
CAP = 4
ITERS = 2
N_BLOCKS = 2048
TILES = 4096
N_SPACE = 8
N_SUB = 2


def draw_force(key, part):
    key = jax.random.fold_in(key, 7)
    first = jax.random.fold_in(key, 0)
    ramp = 1.0 + 2.0 * jnp.arange(N_BLOCKS, dtype=jnp.float32)[:, None] / max(N_BLOCKS - 1, 1)
    values = jnp.clip(jax.random.normal(first, (N_BLOCKS, 6 * BLOCK), jnp.float32), -4.0, 4.0)
    return values * ramp


def draw_mode_matrix(key, part):
    key = jax.random.fold_in(key, 11)
    first, second = jax.random.split(key)
    raw = jax.random.uniform(first, (6, 6), jnp.float32, -1.0, 1.0)
    spread = 0.15
    symmetric = spread * (raw + raw.T)
    identity = jnp.eye(6, dtype=jnp.float32)
    diagonal = 2.0 + jax.random.uniform(second, (6,), jnp.float32, 0.0, 0.9)
    return symmetric * (1.0 - identity) + identity * diagonal[None, :]


def place_ends(array, rng, smallest, largest):
    extent = array.shape
    place = [jax.random.randint(jax.random.fold_in(rng, axis), (), 0, extent[axis]) for axis in range(len(extent))]
    array = array.at[tuple(place)].set(smallest)
    longest = extent.index(max(extent))
    place[longest] = (place[longest] + 1) % extent[longest]
    return array.at[tuple(place)].set(largest)


def shard_levels(stream_key, extent, cuts, low, top_value):
    factor_of = 1.0
    for dim, blocks in cuts:
        draws = jax.random.uniform(jax.random.fold_in(jax.random.fold_in(stream_key, 6), dim), (blocks,), jnp.float32, low / len(cuts), top_value / len(cuts))
        factor_of = factor_of * jnp.repeat(jnp.exp(draws), extent[dim] // blocks).reshape((-1,) + (1,) * (len(extent) - 1 - dim))
    return factor_of


def setup_inputs(seed: int = 0, part: int = 0) -> dict:
    seeds = jax.random.split(jax.random.key(seed), 8)
    own_keys = jax.random.split(jax.random.fold_in(seeds[7], part), 8)
    force = draw_force(jax.random.fold_in(jax.random.fold_in(seeds[7], part), 71), part)
    drag = jnp.clip(0.5 + 1.5 * jax.random.uniform(own_keys[1], (N_BLOCKS, 6 * BLOCK), jnp.float32) ** shard_levels(own_keys[1], (N_BLOCKS, 6 * BLOCK), ((0, 8),), -0.2, 0.2), 0.5, 2.0)
    mode_matrix = draw_mode_matrix(jax.random.fold_in(seeds[7], 71), part)
    tile_rows = place_ends(jax.random.randint(own_keys[3], (TILES,), 0, BLK_DEV), jax.random.fold_in(own_keys[3], 1), 0, BLK_DEV - 1).astype(jnp.int32)
    tile_cols = place_ends(jax.random.randint(own_keys[4], (TILES,), 0, BLK_DEV + N_SPACE * CAP), jax.random.fold_in(own_keys[4], 1), 0, (BLK_DEV + N_SPACE * CAP) - 1).astype(jnp.int32)
    gaps = jnp.clip(jnp.exp(math.log(1.0) - 4.61031033 * jax.random.uniform(own_keys[5], (TILES, BLOCK * BLOCK), jnp.float32) ** shard_levels(own_keys[5], (TILES, BLOCK * BLOCK), ((0, 16),), -0.2, 0.2)), 0.0099487305, 1.0).astype(jnp.bfloat16)
    send_blocks = place_ends(jax.random.randint(own_keys[6], (N_SPACE, N_SPACE, CAP), 0, BLK_DEV), jax.random.fold_in(own_keys[6], 1), 0, BLK_DEV - 1).astype(jnp.int32)
    return dict(force=force, drag=drag, mode_matrix=mode_matrix, tile_rows=tile_rows, tile_cols=tile_cols, gaps=gaps, send_blocks=send_blocks)


coupling = 0.000244140625
gap_shift = 0.05


def block_indices(tile_rows, tile_cols, send_blocks):
    owner = (jnp.arange(TILES, dtype=jnp.int32) // (N_SUB * TILE_DEV)).astype(jnp.int32)
    row_global = owner * BLK_DEV + tile_rows
    offset = jnp.maximum(tile_cols - BLK_DEV, 0)
    source = (offset // CAP).astype(jnp.int32)
    slot = (offset % CAP).astype(jnp.int32)
    remote = send_blocks[source, owner, slot]
    col_global = jnp.where(tile_cols < BLK_DEV, owner * BLK_DEV + tile_cols, source * BLK_DEV + remote)
    return row_global.astype(jnp.int32), col_global.astype(jnp.int32)


def apply_operator(field, drag, mode_matrix, row_global, col_global, gaps):
    groups = TILES // TILE_DEV
    rows_split = row_global.reshape(groups, TILE_DEV)
    cols_split = col_global.reshape(groups, TILE_DEV)
    gaps_split = gaps.reshape(groups, TILE_DEV, BLOCK * BLOCK)

    def step(total, items):
        rows, cols, gap_piece = items
        coeff = coupling / (gap_piece.astype(jnp.float32).reshape(TILE_DEV, BLOCK, BLOCK) + gap_shift)
        row_vals = field[rows].reshape(TILE_DEV, 6, BLOCK)
        col_vals = field[cols].reshape(TILE_DEV, 6, BLOCK)
        row_part = jnp.sum(coeff, axis=2)[:, None, :] * row_vals - jnp.einsum("tpq,tdq->tdp", coeff, col_vals, precision=lax.Precision.HIGHEST)
        col_part = jnp.sum(coeff, axis=1)[:, None, :] * col_vals - jnp.einsum("tpq,tdp->tdq", coeff, row_vals, precision=lax.Precision.HIGHEST)
        total = total.at[rows].add(row_part.reshape(TILE_DEV, 6 * BLOCK))
        total = total.at[cols].add(col_part.reshape(TILE_DEV, 6 * BLOCK))
        return total, None

    start = jnp.zeros((N_BLOCKS, 6 * BLOCK), jnp.float32)
    pairs, unused = lax.scan(step, start, (rows_split, cols_split, gaps_split))
    mixed = jnp.einsum("ij,bjp->bip", mode_matrix, pairs.reshape(N_BLOCKS, 6, BLOCK), precision=lax.Precision.HIGHEST)
    return drag * field + mixed.reshape(N_BLOCKS, 6 * BLOCK)


def reference(force, drag, mode_matrix, tile_rows, tile_cols, gaps, send_blocks):
    row_global, col_global = block_indices(tile_rows, tile_cols, send_blocks)
    velocity = jnp.zeros_like(force)
    residual, direction = force, force
    norm_now = jnp.sum(residual * residual)
    for step in range(ITERS):
        image = apply_operator(direction, drag, mode_matrix, row_global, col_global, gaps)
        alpha = norm_now / jnp.sum(direction * image)
        velocity = velocity + alpha * direction
        residual = residual - alpha * image
        norm_next = jnp.sum(residual * residual)
        direction = residual + (norm_next / norm_now) * direction
        norm_now = norm_next
    return velocity, residual
```

```python
import functools

import jax
import jax.numpy as jnp
from jax import lax
from jax.experimental import pallas as pl
from jax.experimental.pallas import tpu as pltpu
from jax.sharding import PartitionSpec as P

BLOCK = 64
MODES = 6

coupling = 0.000244140625
gap_shift = 0.05

NN = (((1,), (0,)), ((), ()))
NT = (((1,), (1,)), ((), ()))
f32 = jnp.float32
bf16 = jnp.bfloat16


def pieces(x):
    hi = x.astype(bf16)
    rest = x - hi.astype(f32)
    mid = rest.astype(bf16)
    lo = (rest - mid.astype(f32)).astype(bf16)
    return hi, mid, lo


def dot3(x, onehot, dims):
    hi, mid, lo = [
        lax.dot_general(v, onehot, dims, preferred_element_type=f32) for v in pieces(x)
    ]
    return hi + (mid + lo)


def dot3_left(onehot, x, dims):
    hi, mid, lo = [
        lax.dot_general(onehot, v, dims, preferred_element_type=f32) for v in pieces(x)
    ]
    return hi + (mid + lo)


def total(x):
    return jnp.sum(jnp.sum(x, axis=0, keepdims=True), axis=1, keepdims=True)


def kernel(
    n, slots,
    force_ref, drag_ref, mode_ref, rows_ref, cols_ref, exports_ref, gaps_ref,
    vel_ref, res_ref,
    coeff, force_t, drag_t, oh_row, oh_col, oh_halo, oh_exp,
    row_t, col_t, u_row, u_col, image_t, second_t, dir_t, ret_t,
    pad, halo_t, own_send, own_recv,
    h_send, h_recv, t_send, t_recv, a_send, a_recv,
    h_ssem, h_rsem, t_ssem, t_rsem, o_ssem, o_rsem, a_ssem, a_rsem,
):
    me = lax.axis_index("space")
    sub = lax.axis_index("sub")
    other = 1 - sub
    tiles = coeff.shape[1]
    blocks = force_ref.shape[0]
    halo_pad = pad.shape[0]

    barrier = pltpu.get_barrier_semaphore()

    def greet(j, carry):
        peer = lax.rem(me + j, n)
        pl.semaphore_signal(
            barrier, inc=1, device_id={"space": peer, "sub": other},
            device_id_type=pl.DeviceIdType.MESH,
        )

        @pl.when(j > 0)
        def _():
            pl.semaphore_signal(
                barrier, inc=1, device_id={"space": peer, "sub": sub},
                device_id_type=pl.DeviceIdType.MESH,
            )

        return carry

    lax.fori_loop(0, n, greet, 0)

    def remote(src, dst, ssem, rsem, peer, core):
        return pltpu.make_async_remote_copy(
            src_ref=src, dst_ref=dst, send_sem=ssem, recv_sem=rsem,
            device_id={"space": peer, "sub": core},
            device_id_type=pl.DeviceIdType.MESH,
        )

    def peers(start, fn):
        def body(j, carry):
            fn(lax.rem(me + j, n))
            return carry

        lax.fori_loop(start, n, body, 0)

    def h_copy(i, peer, slot):
        return remote(
            h_send.at[i, peer], h_recv.at[i, slot], h_ssem.at[i, peer], h_rsem.at[i, slot],
            peer, sub,
        )

    def a_copy(i, peer, slot):
        return remote(
            a_send.at[i], a_recv.at[i, slot], a_ssem.at[i, peer], a_rsem.at[i, slot],
            peer, sub,
        )

    def t_same(i, peer, slot):
        return remote(
            t_send.at[i, peer], t_recv.at[i, sub, slot],
            t_ssem.at[i, 0, peer], t_rsem.at[i, sub, slot], peer, sub,
        )

    def t_cross(i, peer, slot, half):
        return remote(
            t_send.at[i, peer], t_recv.at[i, half, slot],
            t_ssem.at[i, 1, peer], t_rsem.at[i, half, slot], peer, other,
        )

    def own_copy(i):
        return remote(
            own_send.at[i], own_recv.at[i], o_ssem.at[i], o_rsem.at[i], me, other
        )

    def start_halo(i):
        for q in range(n):
            h_send[i, q] = pad[q * slots:(q + 1) * slots, :]
        h_recv[i, me] = h_send[i, me]

    def finish_halo(i):
        peers(1, lambda peer: h_copy(i, peer, peer).wait_recv())
        for q in range(n):
            pad[q * slots:(q + 1) * slots, :] = h_recv[i, q]

    pad[...] = jnp.zeros_like(pad)
    export_ids = exports_ref[...]
    oh_exp[...] = (
        export_ids == lax.broadcasted_iota(jnp.int32, (halo_pad, blocks), 1)
    ).astype(f32).astype(bf16)
    pad[...] = dot3_left(oh_exp[...], force_ref[...], NN)
    start_halo(0)
    pl.semaphore_wait(barrier, 2 * n - 1)
    peers(1, lambda peer: h_copy(0, peer, me).start())

    force_t[...] = jnp.transpose(force_ref[...])
    drag_t[...] = jnp.transpose(drag_ref[...])
    rows = rows_ref[...]
    cols = cols_ref[...]
    block_ids = lax.broadcasted_iota(jnp.int32, (blocks, tiles), 0)
    oh_row[...] = (rows == block_ids).astype(f32).astype(bf16)
    oh_col[...] = (cols == block_ids).astype(f32).astype(bf16)
    halo_ids = lax.broadcasted_iota(jnp.int32, (halo_pad, tiles), 0) + blocks
    oh_halo[...] = (cols == halo_ids).astype(f32).astype(bf16)
    chunk = 256
    eye = (
        lax.broadcasted_iota(jnp.int32, (chunk, chunk), 0)
        == lax.broadcasted_iota(jnp.int32, (chunk, chunk), 1)
    ).astype(f32).astype(bf16)

    def prepare(j, carry):
        at = pl.ds(pl.multiple_of(j * chunk, chunk), chunk)
        turned = lax.dot_general(eye, gaps_ref[:, at], NT, preferred_element_type=f32)
        coeff[at, :] = coupling / (turned + gap_shift)
        return carry

    lax.fori_loop(0, coeff.shape[0] // chunk, prepare, 0)

    lanes = 128
    groups = tiles // lanes
    pairs_of_modes = MODES // 2

    def apply_tiles(vec):
        row_t[...] = dot3(vec, oh_row[...], NN)
        col_t[...] = dot3(vec, oh_col[...], NN) + dot3(halo_t[...], oh_halo[...], NN)

        def outer(g, carry):
            lane = pl.ds(pl.multiple_of(lax.rem(g, groups) * lanes, lanes), lanes)
            base = (g // groups) * (2 * BLOCK)
            first = pl.ds(pl.multiple_of(base, BLOCK), BLOCK)
            second = pl.ds(pl.multiple_of(base + BLOCK, BLOCK), BLOCK)
            col_a = col_t[first, lane]
            col_b = col_t[second, lane]

            def inner(i, accs):
                acc_a, acc_b = accs
                at_a = pl.ds(pl.multiple_of(base + i * 8, 8), 8)
                at_b = pl.ds(pl.multiple_of(base + BLOCK + i * 8, 8), 8)
                rows_a = row_t[at_a, lane]
                rows_b = row_t[at_b, lane]
                out_a, out_b = [], []
                for k in range(8):
                    c = coeff[pl.ds(pl.multiple_of((i * 8 + k) * BLOCK, BLOCK), BLOCK), lane]
                    w_a = c * (rows_a[k:k + 1, :] - col_a)
                    w_b = c * (rows_b[k:k + 1, :] - col_b)
                    acc_a = acc_a - w_a
                    acc_b = acc_b - w_b
                    out_a.append(jnp.sum(w_a, axis=0, keepdims=True))
                    out_b.append(jnp.sum(w_b, axis=0, keepdims=True))
                u_row[at_a, lane] = jnp.concatenate(out_a, axis=0)
                u_row[at_b, lane] = jnp.concatenate(out_b, axis=0)
                return acc_a, acc_b

            zero = jnp.zeros((BLOCK, lanes), f32)
            acc_a, acc_b = lax.fori_loop(0, BLOCK // 8, inner, (zero, zero))
            u_col[first, lane] = acc_a
            u_col[second, lane] = acc_b
            return carry

        lax.fori_loop(0, groups * pairs_of_modes, outer, 0)

    def send_terms(i):
        halo_terms = dot3(u_col[...], oh_halo[...], NT)
        pad[...] = jnp.transpose(halo_terms)
        for q in range(n):
            t_send[i, q] = pad[q * slots:(q + 1) * slots, :]
        t_recv[i, sub, me] = t_send[i, me]

        def push(peer):
            t_cross(i, peer, me, sub).start()

            @pl.when(peer != me)
            def _():
                t_same(i, peer, me).start()

        peers(0, push)
        own_send[i] = dot3(u_row[...], oh_row[...], NT) + dot3(u_col[...], oh_col[...], NT)
        own_copy(i).start()

    def collect_terms(i):
        def pull(peer):
            t_cross(i, peer, peer, other).wait_recv()

            @pl.when(peer != me)
            def _():
                t_same(i, peer, peer).wait_recv()

        peers(0, pull)
        for q in range(n):
            pad[q * slots:(q + 1) * slots, :] = t_recv[i, 0, q] + t_recv[i, 1, q]
        ret_t[...] = dot3(jnp.transpose(pad[...]), oh_exp[...], NN)
        own_copy(i).wait_recv()

    def operator_rows(i, at, vec_ref):
        spans = [pl.ds(pl.multiple_of(c * BLOCK + at * 8, 8), 8) for c in range(MODES)]
        pair = [
            (own_send[i, span, :] + own_recv[i, span, :]) + ret_t[span, :] for span in spans
        ]
        out = []
        for c in range(MODES):
            mixed = mode_ref[c, 0] * pair[0]
            for k in range(1, MODES):
                mixed = mixed + mode_ref[c, k] * pair[k]
            out.append(drag_t[spans[c], :] * vec_ref[spans[c], :] + mixed)
        return spans, out

    def fold(x):
        acc = x[:, :128]
        for k in range(1, blocks // 128):
            acc = acc + x[:, k * 128:(k + 1) * 128]
        return acc

    def share(i):
        a_recv[i, me] = a_send[i]
        peers(1, lambda peer: a_copy(i, peer, me).start())

    def gather_sums(i):
        peers(1, lambda peer: a_copy(i, peer, peer).wait_recv())
        acc = a_recv[i, 0]
        for q in range(1, n):
            acc = acc + a_recv[i, q]
        return acc

    finish_halo(0)
    halo_t[...] = jnp.transpose(pad[...])
    apply_tiles(force_t[...])
    send_terms(0)
    collect_terms(0)

    def first_image(at, sums):
        norm, dots = sums
        spans, out = operator_rows(0, at, force_t)
        for c in range(MODES):
            v = force_t[spans[c], :]
            image_t[spans[c], :] = out[c]
            norm = norm + v * v
            dots = dots + v * out[c]
        return norm, dots

    zero = jnp.zeros((8, blocks), f32)
    norm, dots = lax.fori_loop(0, BLOCK // 8, first_image, (zero, zero))
    a_send[0, 0:8, :] = fold(norm)
    a_send[0, 8:16, :] = fold(dots)
    share(0)
    pad[...] = dot3_left(oh_exp[...], image_t[...], NT)
    start_halo(1)
    peers(1, lambda peer: h_copy(1, peer, me).start())
    finish_halo(1)
    sums = gather_sums(0)
    norm0 = total(sums[0:8, :])
    alpha0 = norm0 / total(sums[8:16, :])
    halo_t[...] = halo_t[...] - alpha0 * jnp.transpose(pad[...])
    second_t[...] = force_t[...] - alpha0 * image_t[...]
    resid = second_t[...]
    squares = resid * resid
    part = squares[0:8, :]
    for k in range(1, MODES * BLOCK // 8):
        part = part + squares[k * 8:(k + 1) * 8, :]
    a_send[1, 0:8, :] = fold(part)
    a_send[1, 8:16, :] = jnp.zeros((8, 128), f32)
    share(1)

    apply_tiles(second_t[...])
    send_terms(1)
    norm1 = total(gather_sums(1)[0:8, :])
    beta = norm1 / norm0
    collect_terms(1)

    def second_image(at, dots):
        spans, out = operator_rows(1, at, second_t)
        for c in range(MODES):
            image = out[c] + beta * image_t[spans[c], :]
            direction = second_t[spans[c], :] + beta * force_t[spans[c], :]
            image_t[spans[c], :] = image
            dir_t[spans[c], :] = direction
            dots = dots + direction * image
        return dots

    dots = lax.fori_loop(0, BLOCK // 8, second_image, zero)
    a_send[2, 0:8, :] = fold(dots)
    a_send[2, 8:16, :] = jnp.zeros((8, 128), f32)
    share(2)
    alpha1 = norm1 / total(gather_sums(2)[0:8, :])
    vel_ref[...] = jnp.transpose(alpha0 * force_t[...] + alpha1 * dir_t[...])
    res_ref[...] = jnp.transpose(second_t[...] - alpha1 * image_t[...])

    for i in range(2):
        peers(1, lambda peer: h_copy(i, peer, me).wait_send())
        peers(1, lambda peer: t_same(i, peer, me).wait_send())
        peers(0, lambda peer: t_cross(i, peer, me, sub).wait_send())
        own_copy(i).wait_send()
    for i in range(3):
        peers(1, lambda peer: a_copy(i, peer, me).wait_send())


def shards(n, force, drag, mode_matrix, tile_rows, tile_cols, gaps, send_blocks):
    blocks, width = force.shape
    tiles = tile_rows.shape[0]
    slots = send_blocks.shape[2]
    halo = n * slots
    halo_pad = -(-halo // 128) * 128
    exports = jnp.full((halo_pad, 1), -1, jnp.int32).at[:halo, 0].set(send_blocks.reshape(halo))
    vmem = pl.BlockSpec(memory_space=pltpu.VMEM)
    wide = lambda *shape: pltpu.VMEM(shape, f32)
    out = jax.ShapeDtypeStruct((blocks, width), f32)
    return pl.pallas_call(
        functools.partial(kernel, n, slots),
        out_shape=(out, out),
        in_specs=[vmem, vmem, pl.BlockSpec(memory_space=pltpu.SMEM), vmem, vmem, vmem, vmem],
        out_specs=(vmem, vmem),
        scratch_shapes=[
            wide(gaps.shape[1], tiles),
            wide(width, blocks), wide(width, blocks),
            pltpu.VMEM((blocks, tiles), bf16), pltpu.VMEM((blocks, tiles), bf16),
            pltpu.VMEM((halo_pad, tiles), bf16), pltpu.VMEM((halo_pad, blocks), bf16),
            wide(width, tiles), wide(width, tiles), wide(width, tiles), wide(width, tiles),
            wide(width, blocks), wide(width, blocks), wide(width, blocks), wide(width, blocks),
            wide(halo_pad, width), wide(width, halo_pad),
            wide(2, width, blocks), wide(2, width, blocks),
            wide(2, n, slots, width), wide(2, n, slots, width),
            wide(2, n, slots, width), wide(2, 2, n, slots, width),
            wide(3, 16, 128), wide(3, n, 16, 128),
            pltpu.SemaphoreType.DMA((2, n)), pltpu.SemaphoreType.DMA((2, n)),
            pltpu.SemaphoreType.DMA((2, 2, n)), pltpu.SemaphoreType.DMA((2, 2, n)),
            pltpu.SemaphoreType.DMA((2,)), pltpu.SemaphoreType.DMA((2,)),
            pltpu.SemaphoreType.DMA((3, n)), pltpu.SemaphoreType.DMA((3, n)),
        ],
        compiler_params=pltpu.CompilerParams(
            collective_id=0, has_side_effects=True, vmem_limit_bytes=48 * 1024 * 1024
        ),
    )(
        force, drag, mode_matrix, tile_rows.reshape(1, tiles), tile_cols.reshape(1, tiles),
        exports, gaps,
    )


def solution(mesh):
    return jax.shard_map(
        functools.partial(shards, mesh.shape["space"]),
        mesh=mesh,
        in_specs=(
            P(("real", "space"), None),
            P(("real", "space"), None),
            P(),
            P(("real", "space", "sub")),
            P(("real", "space", "sub")),
            P(("real", "space", "sub"), None),
            P(("real", "space"), None, None),
        ),
        out_specs=(P(("real", "space"), None), P(("real", "space"), None)),
        check_vma=False,
    )
```

```python
import functools

import jax
import jax.numpy as jnp
from jax import lax
from jax.experimental import pallas as pl
from jax.experimental.pallas import tpu as pltpu
from jax.sharding import PartitionSpec as P

BLOCK = 64
MODES = 6

coupling = 0.000244140625
gap_shift = 0.05

NN = (((1,), (0,)), ((), ()))
NT = (((1,), (1,)), ((), ()))
f32 = jnp.float32
bf16 = jnp.bfloat16


def pieces(x):
    hi = x.astype(bf16)
    rest = x - hi.astype(f32)
    mid = rest.astype(bf16)
    lo = (rest - mid.astype(f32)).astype(bf16)
    return hi, mid, lo


def dot3(x, onehot, dims):
    hi, mid, lo = [
        lax.dot_general(v, onehot, dims, preferred_element_type=f32) for v in pieces(x)
    ]
    return hi + (mid + lo)


def dot3_left(onehot, x, dims):
    hi, mid, lo = [
        lax.dot_general(onehot, v, dims, preferred_element_type=f32) for v in pieces(x)
    ]
    return hi + (mid + lo)


def total(x):
    return jnp.sum(jnp.sum(x, axis=0, keepdims=True), axis=1, keepdims=True)


def kernel(
    n, slots,
    force_hbm, drag_hbm, mode_ref, rows_hbm, cols_hbm, exports_ref, gaps_hbm,
    vel_ref, res_ref,
    coeff, force_t, drag_t, oh_row, oh_col, oh_halo, oh_exp,
    row_t, col_t, u_row, u_col, image_t, second_t, dir_t, ret_t,
    pad, halo_t, own_send, own_recv,
    h_send, h_recv, t_send, t_recv, a_send, a_recv,
    h_ssem, h_rsem, t_ssem, t_rsem, o_ssem, o_rsem, a_ssem, a_rsem,
    force_ref, drag_ref, rows_ref, cols_ref, gaps_ref, in_sem,
):
    loads = [
        pltpu.make_async_copy(src, dst, in_sem.at[k])
        for k, (src, dst) in enumerate((
            (force_hbm, force_ref), (rows_hbm, rows_ref), (cols_hbm, cols_ref),
            (gaps_hbm, gaps_ref), (drag_hbm, drag_ref),
        ))
    ]
    for load in loads:
        load.start()
    me = lax.axis_index("space")
    sub = lax.axis_index("sub")
    other = 1 - sub
    tiles = coeff.shape[1]
    blocks = force_ref.shape[0]
    halo_pad = pad.shape[0]

    barrier = pltpu.get_barrier_semaphore()

    def greet(j, carry):
        peer = lax.rem(me + j, n)
        pl.semaphore_signal(
            barrier, inc=1, device_id={"space": peer, "sub": other},
            device_id_type=pl.DeviceIdType.MESH,
        )

        @pl.when(j > 0)
        def _():
            pl.semaphore_signal(
                barrier, inc=1, device_id={"space": peer, "sub": sub},
                device_id_type=pl.DeviceIdType.MESH,
            )

        return carry

    lax.fori_loop(0, n, greet, 0)

    def remote(src, dst, ssem, rsem, peer, core):
        return pltpu.make_async_remote_copy(
            src_ref=src, dst_ref=dst, send_sem=ssem, recv_sem=rsem,
            device_id={"space": peer, "sub": core},
            device_id_type=pl.DeviceIdType.MESH,
        )

    def peers(start, fn):
        def body(j, carry):
            fn(lax.rem(me + j, n))
            return carry

        lax.fori_loop(start, n, body, 0)

    def h_copy(i, peer, slot):
        return remote(
            h_send.at[i, peer], h_recv.at[i, slot], h_ssem.at[i, peer], h_rsem.at[i, slot],
            peer, sub,
        )

    def a_copy(i, peer, slot):
        return remote(
            a_send.at[i], a_recv.at[i, slot], a_ssem.at[i, peer], a_rsem.at[i, slot],
            peer, sub,
        )

    def t_same(i, peer, slot):
        return remote(
            t_send.at[i, peer], t_recv.at[i, sub, slot],
            t_ssem.at[i, 0, peer], t_rsem.at[i, sub, slot], peer, sub,
        )

    def t_cross(i, peer, slot, half):
        return remote(
            t_send.at[i, peer], t_recv.at[i, half, slot],
            t_ssem.at[i, 1, peer], t_rsem.at[i, half, slot], peer, other,
        )

    def own_copy(i):
        return remote(
            own_send.at[i], own_recv.at[i], o_ssem.at[i], o_rsem.at[i], me, other
        )

    def start_halo(i):
        for q in range(n):
            h_send[i, q] = pad[q * slots:(q + 1) * slots, :]
        h_recv[i, me] = h_send[i, me]

    def finish_halo(i):
        peers(1, lambda peer: h_copy(i, peer, peer).wait_recv())
        for q in range(n):
            pad[q * slots:(q + 1) * slots, :] = h_recv[i, q]

    pad[...] = jnp.zeros_like(pad)
    export_ids = exports_ref[...]
    oh_exp[...] = (
        export_ids == lax.broadcasted_iota(jnp.int32, (halo_pad, blocks), 1)
    ).astype(f32).astype(bf16)
    loads[0].wait()
    pad[...] = dot3_left(oh_exp[...], force_ref[...], NN)
    start_halo(0)
    pl.semaphore_wait(barrier, 2 * n - 1)
    peers(1, lambda peer: h_copy(0, peer, me).start())

    for load in loads[1:]:
        load.wait()
    force_t[...] = jnp.transpose(force_ref[...])
    drag_t[...] = jnp.transpose(drag_ref[...])
    rows = rows_ref[...]
    cols = cols_ref[...]
    block_ids = lax.broadcasted_iota(jnp.int32, (blocks, tiles), 0)
    oh_row[...] = (rows == block_ids).astype(f32).astype(bf16)
    oh_col[...] = (cols == block_ids).astype(f32).astype(bf16)
    halo_ids = lax.broadcasted_iota(jnp.int32, (halo_pad, tiles), 0) + blocks
    oh_halo[...] = (cols == halo_ids).astype(f32).astype(bf16)
    chunk = 256
    eye = (
        lax.broadcasted_iota(jnp.int32, (chunk, chunk), 0)
        == lax.broadcasted_iota(jnp.int32, (chunk, chunk), 1)
    ).astype(f32).astype(bf16)

    def prepare(j, carry):
        at = pl.ds(pl.multiple_of(j * chunk, chunk), chunk)
        turned = lax.dot_general(eye, gaps_ref[:, at], NT, preferred_element_type=f32)
        coeff[at, :] = coupling / (turned + gap_shift)
        return carry

    lax.fori_loop(0, coeff.shape[0] // chunk, prepare, 0)

    lanes = 128
    groups = tiles // lanes
    pairs_of_modes = MODES // 2

    def apply_tiles(vec):
        row_t[...] = dot3(vec, oh_row[...], NN)
        col_t[...] = dot3(vec, oh_col[...], NN) + dot3(halo_t[...], oh_halo[...], NN)

        def outer(g, carry):
            lane = pl.ds(pl.multiple_of(lax.rem(g, groups) * lanes, lanes), lanes)
            base = (g // groups) * (2 * BLOCK)
            first = pl.ds(pl.multiple_of(base, BLOCK), BLOCK)
            second = pl.ds(pl.multiple_of(base + BLOCK, BLOCK), BLOCK)
            col_a = col_t[first, lane]
            col_b = col_t[second, lane]

            def inner(i, accs):
                acc_a, acc_b = accs
                at_a = pl.ds(pl.multiple_of(base + i * 8, 8), 8)
                at_b = pl.ds(pl.multiple_of(base + BLOCK + i * 8, 8), 8)
                rows_a = row_t[at_a, lane]
                rows_b = row_t[at_b, lane]
                out_a, out_b = [], []
                for k in range(8):
                    c = coeff[pl.ds(pl.multiple_of((i * 8 + k) * BLOCK, BLOCK), BLOCK), lane]
                    w_a = c * (rows_a[k:k + 1, :] - col_a)
                    w_b = c * (rows_b[k:k + 1, :] - col_b)
                    acc_a = acc_a - w_a
                    acc_b = acc_b - w_b
                    out_a.append(jnp.sum(w_a, axis=0, keepdims=True))
                    out_b.append(jnp.sum(w_b, axis=0, keepdims=True))
                u_row[at_a, lane] = jnp.concatenate(out_a, axis=0)
                u_row[at_b, lane] = jnp.concatenate(out_b, axis=0)
                return acc_a, acc_b

            zero = jnp.zeros((BLOCK, lanes), f32)
            acc_a, acc_b = lax.fori_loop(0, BLOCK // 8, inner, (zero, zero))
            u_col[first, lane] = acc_a
            u_col[second, lane] = acc_b
            return carry

        lax.fori_loop(0, groups * pairs_of_modes, outer, 0)

    def send_terms(i):
        halo_terms = dot3(u_col[...], oh_halo[...], NT)
        pad[...] = jnp.transpose(halo_terms)
        for q in range(n):
            t_send[i, q] = pad[q * slots:(q + 1) * slots, :]
        t_recv[i, sub, me] = t_send[i, me]

        def push(peer):
            t_cross(i, peer, me, sub).start()

            @pl.when(peer != me)
            def _():
                t_same(i, peer, me).start()

        peers(0, push)
        own_send[i] = dot3(u_row[...], oh_row[...], NT) + dot3(u_col[...], oh_col[...], NT)
        own_copy(i).start()

    def collect_terms(i):
        def pull(peer):
            t_cross(i, peer, peer, other).wait_recv()

            @pl.when(peer != me)
            def _():
                t_same(i, peer, peer).wait_recv()

        peers(0, pull)
        for q in range(n):
            pad[q * slots:(q + 1) * slots, :] = t_recv[i, 0, q] + t_recv[i, 1, q]
        ret_t[...] = dot3(jnp.transpose(pad[...]), oh_exp[...], NN)
        own_copy(i).wait_recv()

    def operator_rows(i, at, vec_ref):
        spans = [pl.ds(pl.multiple_of(c * BLOCK + at * 8, 8), 8) for c in range(MODES)]
        pair = [
            (own_send[i, span, :] + own_recv[i, span, :]) + ret_t[span, :] for span in spans
        ]
        out = []
        for c in range(MODES):
            mixed = mode_ref[c, 0] * pair[0]
            for k in range(1, MODES):
                mixed = mixed + mode_ref[c, k] * pair[k]
            out.append(drag_t[spans[c], :] * vec_ref[spans[c], :] + mixed)
        return spans, out

    def fold(x):
        acc = x[:, :128]
        for k in range(1, blocks // 128):
            acc = acc + x[:, k * 128:(k + 1) * 128]
        return acc

    def share(i):
        a_recv[i, me] = a_send[i]
        peers(1, lambda peer: a_copy(i, peer, me).start())

    def gather_sums(i):
        peers(1, lambda peer: a_copy(i, peer, peer).wait_recv())
        acc = a_recv[i, 0]
        for q in range(1, n):
            acc = acc + a_recv[i, q]
        return acc

    finish_halo(0)
    halo_t[...] = jnp.transpose(pad[...])
    apply_tiles(force_t[...])
    send_terms(0)
    collect_terms(0)

    def first_image(at, sums):
        norm, dots = sums
        spans, out = operator_rows(0, at, force_t)
        for c in range(MODES):
            v = force_t[spans[c], :]
            image_t[spans[c], :] = out[c]
            norm = norm + v * v
            dots = dots + v * out[c]
        return norm, dots

    zero = jnp.zeros((8, blocks), f32)
    norm, dots = lax.fori_loop(0, BLOCK // 8, first_image, (zero, zero))
    a_send[0, 0:8, :] = fold(norm)
    a_send[0, 8:16, :] = fold(dots)
    share(0)
    pad[...] = dot3_left(oh_exp[...], image_t[...], NT)
    start_halo(1)
    peers(1, lambda peer: h_copy(1, peer, me).start())
    finish_halo(1)
    sums = gather_sums(0)
    norm0 = total(sums[0:8, :])
    alpha0 = norm0 / total(sums[8:16, :])
    halo_t[...] = halo_t[...] - alpha0 * jnp.transpose(pad[...])
    second_t[...] = force_t[...] - alpha0 * image_t[...]
    resid = second_t[...]
    squares = resid * resid
    part = squares[0:8, :]
    for k in range(1, MODES * BLOCK // 8):
        part = part + squares[k * 8:(k + 1) * 8, :]
    a_send[1, 0:8, :] = fold(part)
    a_send[1, 8:16, :] = jnp.zeros((8, 128), f32)
    share(1)

    apply_tiles(second_t[...])
    send_terms(1)
    norm1 = total(gather_sums(1)[0:8, :])
    beta = norm1 / norm0
    collect_terms(1)

    def second_image(at, dots):
        spans, out = operator_rows(1, at, second_t)
        for c in range(MODES):
            image = out[c] + beta * image_t[spans[c], :]
            direction = second_t[spans[c], :] + beta * force_t[spans[c], :]
            image_t[spans[c], :] = image
            dir_t[spans[c], :] = direction
            dots = dots + direction * image
        return dots

    dots = lax.fori_loop(0, BLOCK // 8, second_image, zero)
    a_send[2, 0:8, :] = fold(dots)
    a_send[2, 8:16, :] = jnp.zeros((8, 128), f32)
    share(2)
    alpha1 = norm1 / total(gather_sums(2)[0:8, :])
    vel_ref[...] = jnp.transpose(alpha0 * force_t[...] + alpha1 * dir_t[...])
    res_ref[...] = jnp.transpose(second_t[...] - alpha1 * image_t[...])

    for i in range(2):
        peers(1, lambda peer: h_copy(i, peer, me).wait_send())
        peers(1, lambda peer: t_same(i, peer, me).wait_send())
        peers(0, lambda peer: t_cross(i, peer, me, sub).wait_send())
        own_copy(i).wait_send()
    for i in range(3):
        peers(1, lambda peer: a_copy(i, peer, me).wait_send())


def shards(n, force, drag, mode_matrix, tile_rows, tile_cols, gaps, send_blocks):
    blocks, width = force.shape
    tiles = tile_rows.shape[0]
    slots = send_blocks.shape[2]
    halo = n * slots
    halo_pad = -(-halo // 128) * 128
    exports = jnp.full((halo_pad, 1), -1, jnp.int32).at[:halo, 0].set(send_blocks.reshape(halo))
    vmem = pl.BlockSpec(memory_space=pltpu.VMEM)
    hbm = pl.BlockSpec(memory_space=pl.ANY)
    wide = lambda *shape: pltpu.VMEM(shape, f32)
    out = jax.ShapeDtypeStruct((blocks, width), f32)
    return pl.pallas_call(
        functools.partial(kernel, n, slots),
        out_shape=(out, out),
        in_specs=[hbm, hbm, pl.BlockSpec(memory_space=pltpu.SMEM), hbm, hbm, vmem, hbm],
        out_specs=(vmem, vmem),
        scratch_shapes=[
            wide(gaps.shape[1], tiles),
            wide(width, blocks), wide(width, blocks),
            pltpu.VMEM((blocks, tiles), bf16), pltpu.VMEM((blocks, tiles), bf16),
            pltpu.VMEM((halo_pad, tiles), bf16), pltpu.VMEM((halo_pad, blocks), bf16),
            wide(width, tiles), wide(width, tiles), wide(width, tiles), wide(width, tiles),
            wide(width, blocks), wide(width, blocks), wide(width, blocks), wide(width, blocks),
            wide(halo_pad, width), wide(width, halo_pad),
            wide(2, width, blocks), wide(2, width, blocks),
            wide(2, n, slots, width), wide(2, n, slots, width),
            wide(2, n, slots, width), wide(2, 2, n, slots, width),
            wide(3, 16, 128), wide(3, n, 16, 128),
            pltpu.SemaphoreType.DMA((2, n)), pltpu.SemaphoreType.DMA((2, n)),
            pltpu.SemaphoreType.DMA((2, 2, n)), pltpu.SemaphoreType.DMA((2, 2, n)),
            pltpu.SemaphoreType.DMA((2,)), pltpu.SemaphoreType.DMA((2,)),
            pltpu.SemaphoreType.DMA((3, n)), pltpu.SemaphoreType.DMA((3, n)),
            wide(blocks, width), wide(blocks, width),
            pltpu.VMEM((1, tiles), jnp.int32), pltpu.VMEM((1, tiles), jnp.int32),
            pltpu.VMEM(gaps.shape, gaps.dtype), pltpu.SemaphoreType.DMA((5,)),
        ],
        compiler_params=pltpu.CompilerParams(
            collective_id=0, has_side_effects=True, vmem_limit_bytes=63 * 1024 * 1024
        ),
    )(
        force, drag, mode_matrix, tile_rows.reshape(1, tiles), tile_cols.reshape(1, tiles),
        exports, gaps,
    )


def solution(mesh):
    return jax.shard_map(
        functools.partial(shards, mesh.shape["space"]),
        mesh=mesh,
        in_specs=(
            P(("real", "space"), None),
            P(("real", "space"), None),
            P(),
            P(("real", "space", "sub")),
            P(("real", "space", "sub")),
            P(("real", "space", "sub"), None),
            P(("real", "space"), None, None),
        ),
        out_specs=(P(("real", "space"), None), P(("real", "space"), None)),
        check_vma=False,
    )
```

```python
import functools

import jax
import jax.numpy as jnp
from jax import lax
from jax.experimental import pallas as pl
from jax.experimental.pallas import tpu as pltpu
from jax.sharding import PartitionSpec as P

BLOCK = 64
MODES = 6

coupling = 0.000244140625
gap_shift = 0.05

NN = (((1,), (0,)), ((), ()))
NT = (((1,), (1,)), ((), ()))
f32 = jnp.float32
bf16 = jnp.bfloat16


def pieces(x):
    hi = x.astype(bf16)
    rest = x - hi.astype(f32)
    mid = rest.astype(bf16)
    lo = (rest - mid.astype(f32)).astype(bf16)
    return hi, mid, lo


def dot3(x, onehot, dims):
    hi, mid, lo = [
        lax.dot_general(v, onehot, dims, preferred_element_type=f32) for v in pieces(x)
    ]
    return hi + (mid + lo)


def dot3_left(onehot, x, dims):
    hi, mid, lo = [
        lax.dot_general(onehot, v, dims, preferred_element_type=f32) for v in pieces(x)
    ]
    return hi + (mid + lo)


def total(x):
    return jnp.sum(jnp.sum(x, axis=0, keepdims=True), axis=1, keepdims=True)


def kernel(
    n, slots,
    force_hbm, drag_hbm, mode_ref, rows_hbm, cols_hbm, exports_ref, gaps_hbm,
    vel_ref, res_ref,
    coeff, force_t, drag_t, oh_row, oh_col, oh_halo, oh_exp,
    row_t, col_t, u_row, u_col, image_t, second_t, dir_t, ret_t,
    pad, halo_t, own_send, own_recv,
    h_send, h_recv, t_send, t_recv, a_send, a_recv,
    h_ssem, h_rsem, t_ssem, t_rsem, o_ssem, o_rsem, a_ssem, a_rsem,
    force_ref, drag_ref, rows_ref, cols_ref, gaps_ref, in_sem, oh_wide,
):
    loads = [
        pltpu.make_async_copy(src, dst, in_sem.at[k])
        for k, (src, dst) in enumerate((
            (force_hbm, force_ref), (rows_hbm, rows_ref), (cols_hbm, cols_ref),
            (gaps_hbm, gaps_ref), (drag_hbm, drag_ref),
        ))
    ]
    for load in loads:
        load.start()
    me = lax.axis_index("space")
    sub = lax.axis_index("sub")
    other = 1 - sub
    tiles = coeff.shape[1]
    blocks = force_ref.shape[0]
    halo_pad = pad.shape[0]

    barrier = pltpu.get_barrier_semaphore()

    def greet(j, carry):
        peer = lax.rem(me + j, n)
        pl.semaphore_signal(
            barrier, inc=1, device_id={"space": peer, "sub": other},
            device_id_type=pl.DeviceIdType.MESH,
        )

        @pl.when(j > 0)
        def _():
            pl.semaphore_signal(
                barrier, inc=1, device_id={"space": peer, "sub": sub},
                device_id_type=pl.DeviceIdType.MESH,
            )

        return carry

    lax.fori_loop(0, n, greet, 0)

    def remote(src, dst, ssem, rsem, peer, core):
        return pltpu.make_async_remote_copy(
            src_ref=src, dst_ref=dst, send_sem=ssem, recv_sem=rsem,
            device_id={"space": peer, "sub": core},
            device_id_type=pl.DeviceIdType.MESH,
        )

    def peers(start, fn):
        def body(j, carry):
            fn(lax.rem(me + j, n))
            return carry

        lax.fori_loop(start, n, body, 0)

    def h_copy(i, peer, slot):
        return remote(
            h_send.at[i, peer], h_recv.at[i, slot], h_ssem.at[i, peer], h_rsem.at[i, slot],
            peer, sub,
        )

    def a_copy(i, peer, slot):
        return remote(
            a_send.at[i], a_recv.at[i, slot], a_ssem.at[i, peer], a_rsem.at[i, slot],
            peer, sub,
        )

    def t_same(i, peer, slot):
        return remote(
            t_send.at[i, peer], t_recv.at[i, sub, slot],
            t_ssem.at[i, 0, peer], t_rsem.at[i, sub, slot], peer, sub,
        )

    def t_cross(i, peer, slot, half):
        return remote(
            t_send.at[i, peer], t_recv.at[i, half, slot],
            t_ssem.at[i, 1, peer], t_rsem.at[i, half, slot], peer, other,
        )

    def own_copy(i):
        return remote(
            own_send.at[i], own_recv.at[i], o_ssem.at[i], o_rsem.at[i], me, other
        )

    def start_halo(i):
        for q in range(n):
            h_send[i, q] = pad[q * slots:(q + 1) * slots, :]
        h_recv[i, me] = h_send[i, me]

    def finish_halo(i):
        peers(1, lambda peer: h_copy(i, peer, peer).wait_recv())
        for q in range(n):
            pad[q * slots:(q + 1) * slots, :] = h_recv[i, q]

    pad[...] = jnp.zeros_like(pad)
    oh_wide[...] = jnp.zeros_like(oh_wide)
    lane_ids = lax.broadcasted_iota(jnp.int32, (1, blocks), 1)
    for q in range(n):
        for k in range(slots):
            at = q * slots + k
            oh_wide[at:at + 1, :] = (lane_ids == exports_ref[0, q, k]).astype(f32)
    oh_exp[...] = oh_wide[...].astype(bf16)
    loads[0].wait()
    pad[...] = dot3_left(oh_exp[...], force_ref[...], NN)
    start_halo(0)
    pl.semaphore_wait(barrier, 2 * n - 1)
    peers(1, lambda peer: h_copy(0, peer, me).start())

    for load in loads[1:]:
        load.wait()
    force_t[...] = jnp.transpose(force_ref[...])
    drag_t[...] = jnp.transpose(drag_ref[...])
    rows = rows_ref[...]
    cols = cols_ref[...]
    block_ids = lax.broadcasted_iota(jnp.int32, (blocks, tiles), 0)
    oh_row[...] = (rows == block_ids).astype(f32).astype(bf16)
    oh_col[...] = (cols == block_ids).astype(f32).astype(bf16)
    halo_ids = lax.broadcasted_iota(jnp.int32, (halo_pad, tiles), 0) + blocks
    oh_halo[...] = (cols == halo_ids).astype(f32).astype(bf16)
    chunk = 256
    eye = (
        lax.broadcasted_iota(jnp.int32, (chunk, chunk), 0)
        == lax.broadcasted_iota(jnp.int32, (chunk, chunk), 1)
    ).astype(f32).astype(bf16)

    def prepare(j, carry):
        at = pl.ds(pl.multiple_of(j * chunk, chunk), chunk)
        turned = lax.dot_general(eye, gaps_ref[:, at], NT, preferred_element_type=f32)
        coeff[at, :] = coupling / (turned + gap_shift)
        return carry

    lax.fori_loop(0, coeff.shape[0] // chunk, prepare, 0)

    lanes = 128
    groups = tiles // lanes
    pairs_of_modes = MODES // 2

    def apply_tiles(vec):
        row_t[...] = dot3(vec, oh_row[...], NN)
        col_t[...] = dot3(vec, oh_col[...], NN) + dot3(halo_t[...], oh_halo[...], NN)

        def outer(g, carry):
            lane = pl.ds(pl.multiple_of(lax.rem(g, groups) * lanes, lanes), lanes)
            base = (g // groups) * (2 * BLOCK)
            first = pl.ds(pl.multiple_of(base, BLOCK), BLOCK)
            second = pl.ds(pl.multiple_of(base + BLOCK, BLOCK), BLOCK)
            col_a = col_t[first, lane]
            col_b = col_t[second, lane]

            def inner(i, accs):
                acc_a, acc_b = accs
                at_a = pl.ds(pl.multiple_of(base + i * 8, 8), 8)
                at_b = pl.ds(pl.multiple_of(base + BLOCK + i * 8, 8), 8)
                rows_a = row_t[at_a, lane]
                rows_b = row_t[at_b, lane]
                out_a, out_b = [], []
                for k in range(8):
                    c = coeff[pl.ds(pl.multiple_of((i * 8 + k) * BLOCK, BLOCK), BLOCK), lane]
                    w_a = c * (rows_a[k:k + 1, :] - col_a)
                    w_b = c * (rows_b[k:k + 1, :] - col_b)
                    acc_a = acc_a - w_a
                    acc_b = acc_b - w_b
                    out_a.append(jnp.sum(w_a, axis=0, keepdims=True))
                    out_b.append(jnp.sum(w_b, axis=0, keepdims=True))
                u_row[at_a, lane] = jnp.concatenate(out_a, axis=0)
                u_row[at_b, lane] = jnp.concatenate(out_b, axis=0)
                return acc_a, acc_b

            zero = jnp.zeros((BLOCK, lanes), f32)
            acc_a, acc_b = lax.fori_loop(0, BLOCK // 8, inner, (zero, zero))
            u_col[first, lane] = acc_a
            u_col[second, lane] = acc_b
            return carry

        lax.fori_loop(0, groups * pairs_of_modes, outer, 0)

    def send_terms(i):
        halo_terms = dot3(u_col[...], oh_halo[...], NT)
        pad[...] = jnp.transpose(halo_terms)
        for q in range(n):
            t_send[i, q] = pad[q * slots:(q + 1) * slots, :]
        t_recv[i, sub, me] = t_send[i, me]

        def push(peer):
            t_cross(i, peer, me, sub).start()

            @pl.when(peer != me)
            def _():
                t_same(i, peer, me).start()

        peers(0, push)
        own_send[i] = dot3(u_row[...], oh_row[...], NT) + dot3(u_col[...], oh_col[...], NT)
        own_copy(i).start()

    def collect_terms(i):
        def pull(peer):
            t_cross(i, peer, peer, other).wait_recv()

            @pl.when(peer != me)
            def _():
                t_same(i, peer, peer).wait_recv()

        peers(0, pull)
        for q in range(n):
            pad[q * slots:(q + 1) * slots, :] = t_recv[i, 0, q] + t_recv[i, 1, q]
        ret_t[...] = dot3(jnp.transpose(pad[...]), oh_exp[...], NN)
        own_copy(i).wait_recv()

    def operator_rows(i, at, vec_ref):
        spans = [pl.ds(pl.multiple_of(c * BLOCK + at * 8, 8), 8) for c in range(MODES)]
        pair = [
            (own_send[i, span, :] + own_recv[i, span, :]) + ret_t[span, :] for span in spans
        ]
        out = []
        for c in range(MODES):
            mixed = mode_ref[c, 0] * pair[0]
            for k in range(1, MODES):
                mixed = mixed + mode_ref[c, k] * pair[k]
            out.append(drag_t[spans[c], :] * vec_ref[spans[c], :] + mixed)
        return spans, out

    def fold(x):
        acc = x[:, :128]
        for k in range(1, blocks // 128):
            acc = acc + x[:, k * 128:(k + 1) * 128]
        return acc

    def share(i):
        a_recv[i, me] = a_send[i]
        peers(1, lambda peer: a_copy(i, peer, me).start())

    def gather_sums(i):
        peers(1, lambda peer: a_copy(i, peer, peer).wait_recv())
        acc = a_recv[i, 0]
        for q in range(1, n):
            acc = acc + a_recv[i, q]
        return acc

    finish_halo(0)
    halo_t[...] = jnp.transpose(pad[...])
    apply_tiles(force_t[...])
    send_terms(0)
    collect_terms(0)

    def first_image(at, sums):
        norm, dots = sums
        spans, out = operator_rows(0, at, force_t)
        for c in range(MODES):
            v = force_t[spans[c], :]
            image_t[spans[c], :] = out[c]
            norm = norm + v * v
            dots = dots + v * out[c]
        return norm, dots

    zero = jnp.zeros((8, blocks), f32)
    norm, dots = lax.fori_loop(0, BLOCK // 8, first_image, (zero, zero))
    a_send[0, 0:8, :] = fold(norm)
    a_send[0, 8:16, :] = fold(dots)
    share(0)
    pad[...] = dot3_left(oh_exp[...], image_t[...], NT)
    start_halo(1)
    peers(1, lambda peer: h_copy(1, peer, me).start())
    finish_halo(1)
    sums = gather_sums(0)
    norm0 = total(sums[0:8, :])
    alpha0 = norm0 / total(sums[8:16, :])
    halo_t[...] = halo_t[...] - alpha0 * jnp.transpose(pad[...])
    second_t[...] = force_t[...] - alpha0 * image_t[...]
    resid = second_t[...]
    squares = resid * resid
    part = squares[0:8, :]
    for k in range(1, MODES * BLOCK // 8):
        part = part + squares[k * 8:(k + 1) * 8, :]
    a_send[1, 0:8, :] = fold(part)
    a_send[1, 8:16, :] = jnp.zeros((8, 128), f32)
    share(1)

    apply_tiles(second_t[...])
    send_terms(1)
    norm1 = total(gather_sums(1)[0:8, :])
    beta = norm1 / norm0
    collect_terms(1)

    def second_image(at, dots):
        spans, out = operator_rows(1, at, second_t)
        for c in range(MODES):
            image = out[c] + beta * image_t[spans[c], :]
            direction = second_t[spans[c], :] + beta * force_t[spans[c], :]
            image_t[spans[c], :] = image
            dir_t[spans[c], :] = direction
            dots = dots + direction * image
        return dots

    dots = lax.fori_loop(0, BLOCK // 8, second_image, zero)
    a_send[2, 0:8, :] = fold(dots)
    a_send[2, 8:16, :] = jnp.zeros((8, 128), f32)
    share(2)
    alpha1 = norm1 / total(gather_sums(2)[0:8, :])
    vel_ref[...] = jnp.transpose(alpha0 * force_t[...] + alpha1 * dir_t[...])
    res_ref[...] = jnp.transpose(second_t[...] - alpha1 * image_t[...])

    for i in range(2):
        peers(1, lambda peer: h_copy(i, peer, me).wait_send())
        peers(1, lambda peer: t_same(i, peer, me).wait_send())
        peers(0, lambda peer: t_cross(i, peer, me, sub).wait_send())
        own_copy(i).wait_send()
    for i in range(3):
        peers(1, lambda peer: a_copy(i, peer, me).wait_send())


def shards(n, force, drag, mode_matrix, tile_rows, tile_cols, gaps, send_blocks):
    blocks, width = force.shape
    tiles = tile_rows.shape[0]
    slots = send_blocks.shape[2]
    halo = n * slots
    halo_pad = -(-halo // 128) * 128
    smem = pl.BlockSpec(memory_space=pltpu.SMEM)
    vmem = pl.BlockSpec(memory_space=pltpu.VMEM)
    hbm = pl.BlockSpec(memory_space=pl.ANY)
    wide = lambda *shape: pltpu.VMEM(shape, f32)
    out = pltpu.VMEM((blocks, width), f32)
    return pl.pallas_call(
        functools.partial(kernel, n, slots),
        out_shape=(out, out),
        in_specs=[hbm, hbm, smem, hbm, hbm, smem, hbm],
        out_specs=(vmem, vmem),
        scratch_shapes=[
            wide(gaps.shape[1], tiles),
            wide(width, blocks), wide(width, blocks),
            pltpu.VMEM((blocks, tiles), bf16), pltpu.VMEM((blocks, tiles), bf16),
            pltpu.VMEM((halo_pad, tiles), bf16), pltpu.VMEM((halo_pad, blocks), bf16),
            wide(width, tiles), wide(width, tiles), wide(width, tiles), wide(width, tiles),
            wide(width, blocks), wide(width, blocks), wide(width, blocks), wide(width, blocks),
            wide(halo_pad, width), wide(width, halo_pad),
            wide(2, width, blocks), wide(2, width, blocks),
            wide(2, n, slots, width), wide(2, n, slots, width),
            wide(2, n, slots, width), wide(2, 2, n, slots, width),
            wide(3, 16, 128), wide(3, n, 16, 128),
            pltpu.SemaphoreType.DMA((2, n)), pltpu.SemaphoreType.DMA((2, n)),
            pltpu.SemaphoreType.DMA((2, 2, n)), pltpu.SemaphoreType.DMA((2, 2, n)),
            pltpu.SemaphoreType.DMA((2,)), pltpu.SemaphoreType.DMA((2,)),
            pltpu.SemaphoreType.DMA((3, n)), pltpu.SemaphoreType.DMA((3, n)),
            wide(blocks, width), wide(blocks, width),
            pltpu.VMEM((1, tiles), jnp.int32), pltpu.VMEM((1, tiles), jnp.int32),
            pltpu.VMEM(gaps.shape, gaps.dtype), pltpu.SemaphoreType.DMA((5,)),
            wide(halo_pad, blocks),
        ],
        compiler_params=pltpu.CompilerParams(
            collective_id=0, has_side_effects=True, vmem_limit_bytes=63 * 1024 * 1024
        ),
    )(
        force, drag, mode_matrix, tile_rows.reshape(1, tiles), tile_cols.reshape(1, tiles),
        send_blocks, gaps,
    )


def solution(mesh):
    return jax.shard_map(
        functools.partial(shards, mesh.shape["space"]),
        mesh=mesh,
        in_specs=(
            P(("real", "space"), None),
            P(("real", "space"), None),
            P(),
            P(("real", "space", "sub")),
            P(("real", "space", "sub")),
            P(("real", "space", "sub"), None),
            P(("real", "space"), None, None),
        ),
        out_specs=(P(("real", "space"), None), P(("real", "space"), None)),
        check_vma=False,
    )
```

```python
import functools

import jax
import jax.numpy as jnp
from jax import lax
from jax.experimental import pallas as pl
from jax.experimental.pallas import tpu as pltpu
from jax.sharding import PartitionSpec as P

BLOCK = 64
MODES = 6

coupling = 0.000244140625
gap_shift = 0.05

NN = (((1,), (0,)), ((), ()))
NT = (((1,), (1,)), ((), ()))
f32 = jnp.float32
bf16 = jnp.bfloat16


def pieces(x):
    hi = x.astype(bf16)
    rest = x - hi.astype(f32)
    mid = rest.astype(bf16)
    lo = (rest - mid.astype(f32)).astype(bf16)
    return hi, mid, lo


def dot3(x, onehot, dims):
    hi, mid, lo = [
        lax.dot_general(v, onehot, dims, preferred_element_type=f32) for v in pieces(x)
    ]
    return hi + (mid + lo)


def dot3_left(onehot, x, dims):
    hi, mid, lo = [
        lax.dot_general(onehot, v, dims, preferred_element_type=f32) for v in pieces(x)
    ]
    return hi + (mid + lo)


def fold_rows(w):
    parts = [w[k:k + 8, :] for k in range(0, w.shape[0], 8)]
    while len(parts) > 1:
        parts = [a + b for a, b in zip(parts[::2], parts[1::2])]
    return parts[0]


def row_totals(xs):
    row = lax.broadcasted_iota(jnp.int32, xs[0].shape, 0)
    low = row < 4
    ys = [
        jnp.where(low, a, b) + pltpu.roll(jnp.where(low, b, a), 4, 0)
        for a, b in zip(xs[:4], xs[4:])
    ]
    for step in (2, 1):
        keep = row % (2 * step) < step
        ys = [
            jnp.where(keep, a + pltpu.roll(a, 8 - step, 0), b + pltpu.roll(b, step, 0))
            for a, b in zip(ys[:step], ys[step:])
        ]
    return ys[0]


def total(x):
    return jnp.sum(jnp.sum(x, axis=0, keepdims=True), axis=1, keepdims=True)


def kernel(
    n, slots,
    force_hbm, drag_hbm, mode_ref, rows_hbm, cols_hbm, exports_ref, gaps_hbm,
    vel_ref, res_ref,
    coeff, force_t, drag_t, oh_row, oh_col, oh_halo, oh_exp,
    row_t, col_t, u_row, u_col, image_t, second_t, dir_t, ret_t,
    pad, halo_t, own_send, own_recv,
    h_send, h_recv, t_send, t_recv, a_send, a_recv,
    h_ssem, h_rsem, t_ssem, t_rsem, o_ssem, o_rsem, a_ssem, a_rsem,
    force_ref, drag_ref, rows_ref, cols_ref, gaps_ref, in_sem, oh_wide,
):
    loads = [
        pltpu.make_async_copy(src, dst, in_sem.at[k])
        for k, (src, dst) in enumerate((
            (force_hbm, force_ref), (rows_hbm, rows_ref), (cols_hbm, cols_ref),
            (gaps_hbm, gaps_ref), (drag_hbm, drag_ref),
        ))
    ]
    for load in loads:
        load.start()
    me = lax.axis_index("space")
    sub = lax.axis_index("sub")
    other = 1 - sub
    tiles = coeff.shape[1]
    blocks = force_ref.shape[0]
    halo_pad = pad.shape[0]

    barrier = pltpu.get_barrier_semaphore()

    def greet(j, carry):
        peer = lax.rem(me + j, n)
        pl.semaphore_signal(
            barrier, inc=1, device_id={"space": peer, "sub": other},
            device_id_type=pl.DeviceIdType.MESH,
        )

        @pl.when(j > 0)
        def _():
            pl.semaphore_signal(
                barrier, inc=1, device_id={"space": peer, "sub": sub},
                device_id_type=pl.DeviceIdType.MESH,
            )

        return carry

    lax.fori_loop(0, n, greet, 0)

    def remote(src, dst, ssem, rsem, peer, core):
        return pltpu.make_async_remote_copy(
            src_ref=src, dst_ref=dst, send_sem=ssem, recv_sem=rsem,
            device_id={"space": peer, "sub": core},
            device_id_type=pl.DeviceIdType.MESH,
        )

    def peers(start, fn):
        def body(j, carry):
            fn(lax.rem(me + j, n))
            return carry

        lax.fori_loop(start, n, body, 0)

    def h_copy(i, peer, slot):
        return remote(
            h_send.at[i, peer], h_recv.at[i, slot], h_ssem.at[i, peer], h_rsem.at[i, slot],
            peer, sub,
        )

    def a_copy(i, peer, slot):
        return remote(
            a_send.at[i], a_recv.at[i, slot], a_ssem.at[i, peer], a_rsem.at[i, slot],
            peer, sub,
        )

    def t_same(i, peer, slot):
        return remote(
            t_send.at[i, peer], t_recv.at[i, sub, slot],
            t_ssem.at[i, 0, peer], t_rsem.at[i, sub, slot], peer, sub,
        )

    def t_cross(i, peer, slot, half):
        return remote(
            t_send.at[i, peer], t_recv.at[i, half, slot],
            t_ssem.at[i, 1, peer], t_rsem.at[i, half, slot], peer, other,
        )

    def own_copy(i):
        return remote(
            own_send.at[i], own_recv.at[i], o_ssem.at[i], o_rsem.at[i], me, other
        )

    def start_halo(i):
        for q in range(n):
            h_send[i, q] = pad[q * slots:(q + 1) * slots, :]
        h_recv[i, me] = h_send[i, me]

    def finish_halo(i):
        peers(1, lambda peer: h_copy(i, peer, peer).wait_recv())
        for q in range(n):
            pad[q * slots:(q + 1) * slots, :] = h_recv[i, q]

    pad[...] = jnp.zeros_like(pad)
    oh_wide[...] = jnp.zeros_like(oh_wide)
    lane_ids = lax.broadcasted_iota(jnp.int32, (1, blocks), 1)
    for q in range(n):
        for k in range(slots):
            at = q * slots + k
            oh_wide[at:at + 1, :] = (lane_ids == exports_ref[0, q, k]).astype(f32)
    oh_exp[...] = oh_wide[...].astype(bf16)
    loads[0].wait()
    pad[...] = dot3_left(oh_exp[...], force_ref[...], NN)
    start_halo(0)
    pl.semaphore_wait(barrier, 2 * n - 1)
    peers(1, lambda peer: h_copy(0, peer, me).start())

    for load in loads[1:]:
        load.wait()
    force_t[...] = jnp.transpose(force_ref[...])
    drag_t[...] = jnp.transpose(drag_ref[...])
    rows = rows_ref[...]
    cols = cols_ref[...]
    block_ids = lax.broadcasted_iota(jnp.int32, (blocks, tiles), 0)
    oh_row[...] = (rows == block_ids).astype(f32).astype(bf16)
    oh_col[...] = (cols == block_ids).astype(f32).astype(bf16)
    halo_ids = lax.broadcasted_iota(jnp.int32, (halo_pad, tiles), 0) + blocks
    oh_halo[...] = (cols == halo_ids).astype(f32).astype(bf16)
    chunk = 256
    eye = (
        lax.broadcasted_iota(jnp.int32, (chunk, chunk), 0)
        == lax.broadcasted_iota(jnp.int32, (chunk, chunk), 1)
    ).astype(f32).astype(bf16)

    def prepare(j, carry):
        at = pl.ds(pl.multiple_of(j * chunk, chunk), chunk)
        turned = lax.dot_general(eye, gaps_ref[:, at], NT, preferred_element_type=f32)
        coeff[at, :] = coupling / (turned + gap_shift)
        return carry

    lax.fori_loop(0, coeff.shape[0] // chunk, prepare, 0)

    lanes = 128
    groups = tiles // lanes
    pairs_of_modes = MODES // 2

    def apply_tiles(vec):
        row_t[...] = dot3(vec, oh_row[...], NN)
        col_t[...] = dot3(vec, oh_col[...], NN) + dot3(halo_t[...], oh_halo[...], NN)

        def outer(g, carry):
            lane = pl.ds(pl.multiple_of(lax.rem(g, groups) * lanes, lanes), lanes)
            base = (g // groups) * (2 * BLOCK)
            first = pl.ds(pl.multiple_of(base, BLOCK), BLOCK)
            second = pl.ds(pl.multiple_of(base + BLOCK, BLOCK), BLOCK)
            col_a = col_t[first, lane]
            col_b = col_t[second, lane]

            def inner(i, accs):
                acc_a, acc_b = accs
                at_a = pl.ds(pl.multiple_of(base + i * 8, 8), 8)
                at_b = pl.ds(pl.multiple_of(base + BLOCK + i * 8, 8), 8)
                rows_a = row_t[at_a, lane]
                rows_b = row_t[at_b, lane]
                out_a, out_b = [], []
                for k in range(8):
                    c = coeff[pl.ds(pl.multiple_of((i * 8 + k) * BLOCK, BLOCK), BLOCK), lane]
                    w_a = c * (rows_a[k:k + 1, :] - col_a)
                    w_b = c * (rows_b[k:k + 1, :] - col_b)
                    acc_a = acc_a - w_a
                    acc_b = acc_b - w_b
                    out_a.append(fold_rows(w_a))
                    out_b.append(fold_rows(w_b))
                u_row[at_a, lane] = row_totals(out_a)
                u_row[at_b, lane] = row_totals(out_b)
                return acc_a, acc_b

            zero = jnp.zeros((BLOCK, lanes), f32)
            acc_a, acc_b = lax.fori_loop(0, BLOCK // 8, inner, (zero, zero))
            u_col[first, lane] = acc_a
            u_col[second, lane] = acc_b
            return carry

        lax.fori_loop(0, groups * pairs_of_modes, outer, 0)

    def send_terms(i):
        halo_terms = dot3(u_col[...], oh_halo[...], NT)
        pad[...] = jnp.transpose(halo_terms)
        for q in range(n):
            t_send[i, q] = pad[q * slots:(q + 1) * slots, :]
        t_recv[i, sub, me] = t_send[i, me]

        def push(peer):
            t_cross(i, peer, me, sub).start()

            @pl.when(peer != me)
            def _():
                t_same(i, peer, me).start()

        peers(0, push)
        own_send[i] = dot3(u_row[...], oh_row[...], NT) + dot3(u_col[...], oh_col[...], NT)
        own_copy(i).start()

    def collect_terms(i):
        def pull(peer):
            t_cross(i, peer, peer, other).wait_recv()

            @pl.when(peer != me)
            def _():
                t_same(i, peer, peer).wait_recv()

        peers(0, pull)
        for q in range(n):
            pad[q * slots:(q + 1) * slots, :] = t_recv[i, 0, q] + t_recv[i, 1, q]
        ret_t[...] = dot3(jnp.transpose(pad[...]), oh_exp[...], NN)
        own_copy(i).wait_recv()

    def operator_rows(i, at, vec_ref):
        spans = [pl.ds(pl.multiple_of(c * BLOCK + at * 8, 8), 8) for c in range(MODES)]
        pair = [
            (own_send[i, span, :] + own_recv[i, span, :]) + ret_t[span, :] for span in spans
        ]
        out = []
        for c in range(MODES):
            mixed = mode_ref[c, 0] * pair[0]
            for k in range(1, MODES):
                mixed = mixed + mode_ref[c, k] * pair[k]
            out.append(drag_t[spans[c], :] * vec_ref[spans[c], :] + mixed)
        return spans, out

    def fold(x):
        acc = x[:, :128]
        for k in range(1, blocks // 128):
            acc = acc + x[:, k * 128:(k + 1) * 128]
        return acc

    def share(i):
        a_recv[i, me] = a_send[i]
        peers(1, lambda peer: a_copy(i, peer, me).start())

    def gather_sums(i):
        peers(1, lambda peer: a_copy(i, peer, peer).wait_recv())
        acc = a_recv[i, 0]
        for q in range(1, n):
            acc = acc + a_recv[i, q]
        return acc

    finish_halo(0)
    halo_t[...] = jnp.transpose(pad[...])
    apply_tiles(force_t[...])
    send_terms(0)
    collect_terms(0)

    def first_image(at, sums):
        norm, dots = sums
        spans, out = operator_rows(0, at, force_t)
        for c in range(MODES):
            v = force_t[spans[c], :]
            image_t[spans[c], :] = out[c]
            norm = norm + v * v
            dots = dots + v * out[c]
        return norm, dots

    zero = jnp.zeros((8, blocks), f32)
    norm, dots = lax.fori_loop(0, BLOCK // 8, first_image, (zero, zero))
    a_send[0, 0:8, :] = fold(norm)
    a_send[0, 8:16, :] = fold(dots)
    share(0)
    pad[...] = dot3_left(oh_exp[...], image_t[...], NT)
    start_halo(1)
    peers(1, lambda peer: h_copy(1, peer, me).start())
    finish_halo(1)
    sums = gather_sums(0)
    norm0 = total(sums[0:8, :])
    alpha0 = norm0 / total(sums[8:16, :])
    halo_t[...] = halo_t[...] - alpha0 * jnp.transpose(pad[...])
    second_t[...] = force_t[...] - alpha0 * image_t[...]
    resid = second_t[...]
    squares = resid * resid
    part = squares[0:8, :]
    for k in range(1, MODES * BLOCK // 8):
        part = part + squares[k * 8:(k + 1) * 8, :]
    a_send[1, 0:8, :] = fold(part)
    a_send[1, 8:16, :] = jnp.zeros((8, 128), f32)
    share(1)

    apply_tiles(second_t[...])
    send_terms(1)
    norm1 = total(gather_sums(1)[0:8, :])
    beta = norm1 / norm0
    collect_terms(1)

    def second_image(at, dots):
        spans, out = operator_rows(1, at, second_t)
        for c in range(MODES):
            image = out[c] + beta * image_t[spans[c], :]
            direction = second_t[spans[c], :] + beta * force_t[spans[c], :]
            image_t[spans[c], :] = image
            dir_t[spans[c], :] = direction
            dots = dots + direction * image
        return dots

    dots = lax.fori_loop(0, BLOCK // 8, second_image, zero)
    a_send[2, 0:8, :] = fold(dots)
    a_send[2, 8:16, :] = jnp.zeros((8, 128), f32)
    share(2)
    alpha1 = norm1 / total(gather_sums(2)[0:8, :])
    vel_ref[...] = jnp.transpose(alpha0 * force_t[...] + alpha1 * dir_t[...])
    res_ref[...] = jnp.transpose(second_t[...] - alpha1 * image_t[...])

    for i in range(2):
        peers(1, lambda peer: h_copy(i, peer, me).wait_send())
        peers(1, lambda peer: t_same(i, peer, me).wait_send())
        peers(0, lambda peer: t_cross(i, peer, me, sub).wait_send())
        own_copy(i).wait_send()
    for i in range(3):
        peers(1, lambda peer: a_copy(i, peer, me).wait_send())


def shards(n, force, drag, mode_matrix, tile_rows, tile_cols, gaps, send_blocks):
    blocks, width = force.shape
    tiles = tile_rows.shape[0]
    slots = send_blocks.shape[2]
    halo = n * slots
    halo_pad = -(-halo // 128) * 128
    smem = pl.BlockSpec(memory_space=pltpu.SMEM)
    vmem = pl.BlockSpec(memory_space=pltpu.VMEM)
    hbm = pl.BlockSpec(memory_space=pl.ANY)
    wide = lambda *shape: pltpu.VMEM(shape, f32)
    out = pltpu.VMEM((blocks, width), f32)
    return pl.pallas_call(
        functools.partial(kernel, n, slots),
        out_shape=(out, out),
        in_specs=[hbm, hbm, smem, hbm, hbm, smem, hbm],
        out_specs=(vmem, vmem),
        scratch_shapes=[
            wide(gaps.shape[1], tiles),
            wide(width, blocks), wide(width, blocks),
            pltpu.VMEM((blocks, tiles), bf16), pltpu.VMEM((blocks, tiles), bf16),
            pltpu.VMEM((halo_pad, tiles), bf16), pltpu.VMEM((halo_pad, blocks), bf16),
            wide(width, tiles), wide(width, tiles), wide(width, tiles), wide(width, tiles),
            wide(width, blocks), wide(width, blocks), wide(width, blocks), wide(width, blocks),
            wide(halo_pad, width), wide(width, halo_pad),
            wide(2, width, blocks), wide(2, width, blocks),
            wide(2, n, slots, width), wide(2, n, slots, width),
            wide(2, n, slots, width), wide(2, 2, n, slots, width),
            wide(3, 16, 128), wide(3, n, 16, 128),
            pltpu.SemaphoreType.DMA((2, n)), pltpu.SemaphoreType.DMA((2, n)),
            pltpu.SemaphoreType.DMA((2, 2, n)), pltpu.SemaphoreType.DMA((2, 2, n)),
            pltpu.SemaphoreType.DMA((2,)), pltpu.SemaphoreType.DMA((2,)),
            pltpu.SemaphoreType.DMA((3, n)), pltpu.SemaphoreType.DMA((3, n)),
            wide(blocks, width), wide(blocks, width),
            pltpu.VMEM((1, tiles), jnp.int32), pltpu.VMEM((1, tiles), jnp.int32),
            pltpu.VMEM(gaps.shape, gaps.dtype), pltpu.SemaphoreType.DMA((5,)),
            wide(halo_pad, blocks),
        ],
        compiler_params=pltpu.CompilerParams(
            collective_id=0, has_side_effects=True, vmem_limit_bytes=63 * 1024 * 1024
        ),
    )(
        force, drag, mode_matrix, tile_rows.reshape(1, tiles), tile_cols.reshape(1, tiles),
        send_blocks, gaps,
    )


def solution(mesh):
    return jax.shard_map(
        functools.partial(shards, mesh.shape["space"]),
        mesh=mesh,
        in_specs=(
            P(("real", "space"), None),
            P(("real", "space"), None),
            P(),
            P(("real", "space", "sub")),
            P(("real", "space", "sub")),
            P(("real", "space", "sub"), None),
            P(("real", "space"), None, None),
        ),
        out_specs=(P(("real", "space"), None), P(("real", "space"), None)),
        check_vma=False,
    )
```
